32 devices in a mesh: wide: 8 (over z, core), narrow: 4 (over y, x).
Axes of the slice: x: 2, y: 2, z: 4, core: 2. Of those that a mesh axis runs over, the one named last changes fastest.
Arguments:
- scalar_field: float32 [128, 256, 2048], P('wide', 'narrow'), may hold values from -6 to 6
- depth_rank: int32 [8], replicated, may hold values from 0 to 7, each once
- transfer: float32 [2, 3], replicated, may hold values from -2 to 2
- light_dir: float32 [3], replicated, may hold values from -1 to 1
Outputs:
- final_image: float32 [3, 256, 2048], P(None, 'narrow')
The draws below stay inside these ranges and needn't reach their ends.
Inputs may be any that keep to these rules, and one draw needn't show every extreme that they name: `depth_rank`: every rank 0 to 7 appears exactly once.
All inputs are finite; a program needn't handle non-finite values.
Results may differ from the reference program's by a relative error of at most 0.000067.
Values sent between devices are 32-bit elements; how exact they have to be, the bound alone decides.
No kernel may reach another device: no remote copies, remote signals or barrier semaphores. Data moves between devices by JAX's collectives and lax.ppermute only.
A program may use at most 128 MiB of HBM per device.

```python
import jax
import jax.numpy as jnp
from jax import lax

COLS = 2048
PLANES = 16
ROWS = 256
NZ = 128
N_WIDE = 8


def level_of(stream_key, extent, pieces, least, high):
    loudness = 1.0
    for dim, shards_of in pieces:
        steps = jax.random.uniform(jax.random.fold_in(jax.random.fold_in(stream_key, 6), dim), (shards_of,), jnp.float32, least / len(pieces), high / len(pieces))
        loudness = loudness * jnp.repeat(jnp.exp(steps), extent[dim] // shards_of).reshape((-1,) + (1,) * (len(extent) - 1 - dim))
    return loudness


def centred(rng, extent, spread, bound, cuts=(), kind=jnp.bfloat16):
    entries = spread * jax.random.normal(rng, extent, jnp.float32)
    if cuts:
        entries = entries * level_of(rng, extent, cuts, -0.22, 0.18)
    return jnp.clip(entries, -bound, bound).astype(kind)


def setup_inputs(seed: int = 0) -> dict:
    keys = jax.random.split(jax.random.key(seed), 5)
    scalar_field = centred(keys[0], (NZ, ROWS, COLS), 1.0, 6.0, ((0, 8), (1, 4)), jnp.float32)
    depth_rank = jax.random.permutation(keys[1], N_WIDE).astype(jnp.int32)
    transfer = jnp.clip(jax.random.uniform(keys[2], (2, 3), jnp.float32, -2.0, 2.0), -2.0, 2.0)
    light_dir = jnp.clip(jax.random.uniform(keys[3], (3,), jnp.float32, -1.0, 1.0), -1.0, 1.0)
    return dict(scalar_field=scalar_field, depth_rank=depth_rank, transfer=transfer, light_dir=light_dir)


background = 0.25
optical_total = 2.0


def march_steps(volume, plane_total):
    return jax.nn.softplus(2.0 * volume) * (optical_total / plane_total)


def render(padded, optical_step, light_dir, transfer):
    volume = padded[:, 1:-1, :]
    shifted_up = jnp.concatenate([volume[:1], volume[:-1]], axis=0)
    shifted_down = jnp.concatenate([volume[1:], volume[-1:]], axis=0)
    slope_depth = (shifted_down - shifted_up) * 0.5
    slope_rows = (padded[:, 2:, :] - padded[:, :-2, :]) * 0.5
    zero_column = jnp.zeros_like(volume[:, :, :1])
    right_cells = jnp.concatenate([volume[:, :, 1:], zero_column], axis=2)
    left_cells = jnp.concatenate([zero_column, volume[:, :, :-1]], axis=2)
    slope_cols = (right_cells - left_cells) * 0.5
    shading = 0.5 + 0.5 * jnp.tanh(light_dir[0] * slope_depth + light_dir[1] * slope_rows + light_dir[2] * slope_cols)
    passed = jnp.cumsum(optical_step, axis=0) - optical_step
    weights = jnp.exp(-passed) * (1.0 - jnp.exp(-optical_step)) * shading
    colors = jax.nn.sigmoid(transfer[0][:, None, None, None] * volume[None] + transfer[1][:, None, None, None])
    return jnp.sum(weights[None] * colors, axis=1)


def reference(scalar_field, depth_rank, transfer, light_dir):
    bricks = scalar_field.reshape(N_WIDE, PLANES, ROWS, COLS)

    def one_brick(volume):
        padded = jnp.pad(volume, ((0, 0), (1, 1), (0, 0)))
        optical_step = march_steps(volume, NZ)
        return render(padded, optical_step, light_dir, transfer), jnp.sum(optical_step, axis=0)

    shaded_color, brick_depth = lax.map(one_brick, bricks)
    in_front = (depth_rank[None, :] < depth_rank[:, None]).astype(jnp.float32)
    front_depth = jnp.einsum("ab,byx->ayx", in_front, brick_depth, precision=lax.Precision.HIGHEST)
    total_depth = jnp.sum(brick_depth, axis=0)
    return jnp.sum(jnp.exp(-front_depth)[:, None] * shaded_color, axis=0) + background * jnp.exp(-total_depth)
```

```python
import functools

import jax
import jax.numpy as jnp
from jax import lax
from jax.experimental import pallas as pl
from jax.experimental.pallas import tpu as pltpu
from jax.sharding import PartitionSpec as P

background = 0.25
optical_total = 2.0

SUB = 8
LANE = 128
GROUP = 256
CHUNKS = (4, 4)


def render_kernel(
    chips, cores, chunk, scale,
    where_ref, transfer_ref, light_ref, field_ref, above_ref, below_ref, *rest
):
    out_refs, (padded, sem) = rest[:chips], rest[chips:]
    planes, rows, columns = field_ref.shape
    start, width = chunk
    tiles = rows // SUB
    parts = chips * cores // tiles
    part = width // parts
    my_chip, my_core = where_ref[0], where_ref[1]

    lead = LANE if start > 0 else 0
    trail = LANE if start + width < columns else 0
    first_tile = lax.rem(my_chip * cores, tiles)

    def copy_of(step):
        tile = lax.rem(first_tile + step, tiles)
        return pltpu.make_async_copy(
            field_ref.at[:, pl.ds(pl.multiple_of(tile * SUB, SUB), SUB), pl.ds(start - lead, lead + width + trail)],
            padded.at[
                :, pl.ds(pl.multiple_of(tile * SUB + SUB, SUB), SUB), pl.ds(LANE - lead, lead + width + trail)
            ],
            sem.at[step],
        )

    for step in range(tiles):
        copy_of(step).start()
    if not lead:
        padded[:, :, :LANE] = jnp.zeros((planes, rows + 2 * SUB, LANE), jnp.float32)
    if not trail:
        padded[:, :, LANE + width :] = jnp.zeros((planes, rows + 2 * SUB, LANE), jnp.float32)
    padded[:, SUB - 1 : SUB, LANE : LANE + width] = above_ref[:, :, start : start + width]
    padded[:, SUB + rows : SUB + rows + 1, LANE : LANE + width] = below_ref[:, :, start : start + width]

    light = [0.5 * light_ref[i] for i in range(3)]
    slope = [0.5 * transfer_ref[0, c] for c in range(3)]
    offset = [0.5 * transfer_ref[1, c] for c in range(3)]
    sub = lax.broadcasted_iota(jnp.int32, (SUB, LANE), 0)
    lane = lax.broadcasted_iota(jnp.int32, (SUB, LANE), 1)
    top, bottom = sub == 0, sub == SUB - 1
    leftmost, rightmost = lane == 0, lane == LANE - 1
    per_group = GROUP // LANE
    groups = part // GROUP

    for step in range(tiles):
        copy_of(step).wait()

    for k in range(chips):
        chip = lax.rem(my_chip + k, chips)
        out_ref = out_refs[k]

        def march(index, carry, chip=chip, out_ref=out_ref):
            relative = index // groups
            column = (index - relative * groups) * GROUP
            owner = chip * cores + lax.rem(my_core + relative, cores)
            tile = lax.rem(owner, tiles)
            row = pl.multiple_of(tile * SUB + SUB, SUB)
            at = pl.multiple_of(LANE + (owner // tiles) * part + column, LANE)

            def load(plane, row_shift, vreg):
                return padded[
                    plane,
                    pl.ds(pl.multiple_of(row + row_shift * SUB, SUB), SUB),
                    pl.ds(pl.multiple_of(at + vreg * LANE, LANE), LANE),
                ]

            zero = jnp.zeros((SUB, LANE), jnp.float32)
            depth = [zero] * per_group
            left_over = [zero + 1.0] * per_group
            total = [zero] * per_group
            sums = [[zero] * per_group for _ in range(3)]
            here = [load(0, 0, v) for v in range(-1, per_group + 1)]
            before = here
            for plane in range(planes):
                after = [load(plane + 1, 0, v) for v in range(-1, per_group + 1)] if plane + 1 < planes else here
                for v in range(per_group):
                    value = here[v + 1]
                    up = pltpu.roll(jnp.where(bottom, load(plane, -1, v), value), 1, 0)
                    down = pltpu.roll(jnp.where(top, load(plane, 1, v), value), SUB - 1, 0)
                    left = pltpu.roll(jnp.where(rightmost, here[v], value), 1, 1)
                    right = pltpu.roll(jnp.where(leftmost, here[v + 2], value), LANE - 1, 1)
                    shade = jnp.tanh(
                        light[0] * (after[v + 1] - before[v + 1]) + light[1] * (down - up) + light[2] * (right - left)
                    )
                    depth[v] = depth[v] + jnp.log(1.0 + jnp.exp(value + value))
                    through = jnp.exp(depth[v] * -scale)
                    lost = left_over[v] - through
                    left_over[v] = through
                    weight = lost + lost * shade
                    total[v] = total[v] + weight
                    for c in range(3):
                        sums[c][v] = sums[c][v] + weight * jnp.tanh(slope[c] * value + offset[c])
                before, here = here, after
            for v in range(per_group):
                lanes = pl.ds(pl.multiple_of(column + v * LANE, LANE), LANE)
                for c in range(3):
                    out_ref[relative, c, :, lanes] = 0.25 * (total[v] + sums[c][v])
                out_ref[relative, 3, :, lanes] = depth[v] * scale
            return carry

        lax.fori_loop(0, cores * groups, march, 0)


def composite_kernel(chips, cores, where_ref, rank_ref, *refs):
    own, other, out_ref = refs[:chips], refs[chips : 2 * chips], refs[2 * chips]
    my_chip, my_core = where_ref[0], where_ref[1]
    blocks, ranks = [], []
    for k in range(chips):
        chip = lax.rem(my_chip + chips - k, chips)
        for core, ref in ((my_core, own[k]), (cores - 1 - my_core, other[k])):
            blocks.append(ref)
            ranks.append(rank_ref[chip * cores + core])
    count = len(blocks)
    ahead = [[(ranks[j] < ranks[i]).astype(jnp.float32) for j in range(count)] for i in range(count)]

    def one(step, carry):
        lanes = pl.ds(pl.multiple_of(step * LANE, LANE), LANE)
        depths = [ref[0, 3, :, lanes] for ref in blocks]
        total = functools.reduce(jnp.add, depths)
        sums = [background * jnp.exp(-total)] * 3
        for i in range(count):
            front = functools.reduce(jnp.add, [ahead[i][j] * depths[j] for j in range(count) if j != i])
            weight = jnp.exp(-front)
            for c in range(3):
                sums[c] = sums[c] + weight * blocks[i][0, c, :, lanes]
        for c in range(3):
            out_ref[c, :, lanes] = sums[c]
        return carry

    lax.fori_loop(0, out_ref.shape[2] // LANE, one, 0)


def place_kernel(chips, cores, tiles, chunks, where_ref, *refs):
    count = len(chunks) * chips * 2
    blocks, out_ref, sem = refs[:count], refs[count], refs[count + 1]
    my_chip, my_core = where_ref[0], where_ref[1]
    copies = []
    for i, (start, width) in enumerate(chunks):
        part = width // (chips * cores // tiles)
        for k in range(chips):
            chip = lax.rem(my_chip + chips - k, chips)
            for j, core in enumerate((my_core, cores - 1 - my_core)):
                owner = chip * cores + core
                row = pl.multiple_of(lax.rem(owner, tiles) * SUB, SUB)
                column = pl.multiple_of(start + (owner // tiles) * part, LANE)
                n = (i * chips + k) * 2 + j
                copy = pltpu.make_async_copy(
                    blocks[n], out_ref.at[:, pl.ds(row, SUB), pl.ds(column, part)], sem.at[n]
                )
                copy.start()
                copies.append(copy)
    for copy in copies:
        copy.wait()


def body(scalar_field, depth_rank, transfer, light_dir):
    planes, rows, columns = scalar_field.shape
    wide, narrow = lax.axis_size("wide"), lax.axis_size("narrow")
    cores = 2
    chips = wide // cores
    tiles = rows // SUB
    parts = wide // tiles
    scale = optical_total / (planes * wide)
    index = lax.axis_index("wide")
    where = jnp.stack([index // cores, index % cores]).astype(jnp.int32)
    chunks, start = [], 0
    for eighths in CHUNKS:
        chunks.append((start, columns * eighths // sum(CHUNKS)))
        start += chunks[-1][1]

    def swap(value):
        return lax.ppermute(value, "wide", [(i, i ^ 1) for i in range(wide)])

    def send(value, k):
        return lax.ppermute(value, "wide", [(i, (i + k * cores) % wide) for i in range(wide)])

    up = [(i, i + 1) for i in range(narrow - 1)]
    above = lax.ppermute(scalar_field[:, rows - 1 :, :], "narrow", up)
    below = lax.ppermute(scalar_field[:, :1, :], "narrow", [(j, i) for i, j in up])

    smem = pl.BlockSpec(memory_space=pltpu.SMEM)
    vmem = pl.BlockSpec(memory_space=pltpu.VMEM)
    anywhere = pl.BlockSpec(memory_space=pl.ANY)
    cells = planes * rows * columns

    finished = []
    for chunk in chunks:
        width = chunk[1]
        part = width // parts
        share = width / columns
        blocks = pl.pallas_call(
            functools.partial(render_kernel, chips, cores, chunk, scale),
            out_shape=[jax.ShapeDtypeStruct((cores, 4, SUB, part), jnp.float32)] * chips,
            in_specs=[smem, smem, smem, anywhere, vmem, vmem],
            out_specs=[vmem] * chips,
            scratch_shapes=[
                pltpu.VMEM((planes, rows + 2 * SUB, width + 2 * LANE), jnp.float32),
                pltpu.SemaphoreType.DMA((tiles,)),
            ],
            cost_estimate=pl.CostEstimate(
                flops=int(40 * cells * share), bytes_accessed=int(6 * cells * share),
                transcendentals=int(7 * cells * share),
            ),
            compiler_params=pltpu.CompilerParams(vmem_limit_bytes=40 * 2**20),
            name="render",
        )(where, transfer, light_dir, scalar_field, above, below)
        own = [blocks[0]] + [send(blocks[k], k) for k in range(1, chips)]
        other = [swap(value) for value in own]
        pick = [pl.BlockSpec((1, 4, SUB, part), functools.partial(lambda r, i: (r, 0, 0, 0), r)) for r in (0, 1)]
        tile = pl.pallas_call(
            functools.partial(composite_kernel, chips, cores),
            grid=(1,),
            out_shape=jax.ShapeDtypeStruct((3, SUB, part), jnp.float32),
            in_specs=[smem, smem] + [pick[0]] * chips + [pick[1]] * chips,
            out_specs=pl.BlockSpec((3, SUB, part), lambda i: (0, 0, 0)),
            cost_estimate=pl.CostEstimate(
                flops=wide * wide * SUB * part * 2, bytes_accessed=wide * 16 * SUB * part,
                transcendentals=wide * SUB * part,
            ),
            compiler_params=pltpu.CompilerParams(vmem_limit_bytes=40 * 2**20),
            name="composite",
        )(where, depth_rank, *own, *other)
        mine = [tile] + [send(tile, k) for k in range(1, chips)]
        for value in mine:
            finished += [value, swap(value)]

    return pl.pallas_call(
        functools.partial(place_kernel, chips, cores, tiles, chunks),
        out_shape=jax.ShapeDtypeStruct((3, rows, columns), jnp.float32),
        in_specs=[smem] + [anywhere] * len(finished),
        out_specs=anywhere,
        scratch_shapes=[pltpu.SemaphoreType.DMA((len(finished),))],
        cost_estimate=pl.CostEstimate(flops=0, bytes_accessed=24 * rows * columns, transcendentals=0),
        name="place",
    )(where, *finished)


def solution(mesh):
    return jax.shard_map(
        body,
        mesh=mesh,
        in_specs=(P("wide", "narrow", None), P(), P(), P()),
        out_specs=P(None, "narrow", None),
        check_vma=False,
    )
```

```python
import functools

import jax
import jax.numpy as jnp
from jax import lax
from jax.experimental import pallas as pl
from jax.experimental.pallas import tpu as pltpu
from jax.sharding import PartitionSpec as P

background = 0.25
optical_total = 2.0

SUB = 8
LANE = 128
CORES = 2
INNER = ((1, 3), (4, 3))
VMEM_LIMIT = 24 * 2**20


def call(kernel, operands, specs, events=(), **options):
    def with_events(*refs):
        kernel(*refs[: len(operands)], *refs[len(operands) + len(events) :])

    return pl.pallas_call(
        with_events,
        in_specs=specs + [pl.BlockSpec(memory_space=pl.ANY)] * len(events),
        compiler_params=pltpu.CompilerParams(vmem_limit_bytes=VMEM_LIMIT),
        **options,
    )(*operands, *events)


def lasting(microseconds):
    return pl.CostEstimate(flops=0, bytes_accessed=int(microseconds * 3.69e6), transcendentals=0)


def tiles_of(runs):
    return sum(number for _, number in runs)


def edges_kernel(field_ref, first_ref, last_ref, buffer, sem):
    rows = field_ref.shape[1]
    copies = [
        pltpu.make_async_copy(field_ref.at[:, pl.ds(row, SUB), :], buffer.at[i], sem.at[i])
        for i, row in enumerate((0, rows - SUB))
    ]
    for copy in copies:
        copy.start()
    for copy in copies:
        copy.wait()
    first_ref[...] = buffer[0, :, :1, :]
    last_ref[...] = buffer[1, :, SUB - 1 :, :]


def render_kernel(runs, tiles, chips, scale, where_ref, transfer_ref, light_ref, field_ref, *refs):
    out_refs, (padded, sem) = refs[-2 - chips : -2], refs[-2:]
    edges = list(refs[: -2 - chips])
    planes, _, columns = field_ref.shape
    part = out_refs[0].shape[3]
    my_chip, my_core = where_ref[0], where_ref[1]

    def tile_copy(tile, slot):
        return pltpu.make_async_copy(
            field_ref.at[:, pl.ds(pl.multiple_of(tile * SUB, SUB), SUB), :],
            padded.at[:, pl.ds(pl.multiple_of(slot * SUB, SUB), SUB), pl.ds(LANE, columns)],
            sem.at[slot],
        )

    layout, slot, written = [], 0, 0
    for first, number in runs:
        low, high = max(first - 1, 0), min(first + number + 1, tiles)
        before = edges.pop(0) if first == 0 else None
        behind = edges.pop(0) if first + number == tiles else None
        layout.append((first, number, low, high, slot, written, before, behind))
        for tile in range(low, high):
            tile_copy(tile, slot + tile - low).start()
        slot, written = slot + high - low, written + number
    rim = jnp.zeros((planes, padded.shape[1], LANE), jnp.float32)
    padded[:, :, :LANE] = rim
    padded[:, :, LANE + columns :] = rim

    light = [0.5 * light_ref[i] for i in range(3)]
    slope = [0.5 * transfer_ref[0, c] for c in range(3)]
    offset = [0.5 * transfer_ref[1, c] for c in range(3)]
    sub = lax.broadcasted_iota(jnp.int32, (SUB, LANE), 0)
    lane = lax.broadcasted_iota(jnp.int32, (SUB, LANE), 1)
    top, bottom = sub == 0, sub == SUB - 1
    leftmost, rightmost = lane == 0, lane == LANE - 1
    vregs = part // LANE

    def march(slot, out_row, before_ref, behind_ref, column, relative, out_ref):
        def load(plane, shift, vreg):
            ref = {-1: before_ref, 1: behind_ref}.get(shift)
            if ref is not None:
                lanes = pl.ds(pl.multiple_of(column + vreg * LANE, LANE), LANE)
                return jnp.broadcast_to(ref[plane, :, lanes], (SUB, LANE))
            return padded[
                plane,
                pl.ds(pl.multiple_of((slot + shift) * SUB, SUB), SUB),
                pl.ds(pl.multiple_of(column + (1 + vreg) * LANE, LANE), LANE),
            ]

        zero = jnp.zeros((SUB, LANE), jnp.float32)
        depth = [zero] * vregs
        left_over = [zero + 1.0] * vregs
        total = [zero] * vregs
        sums = [[zero] * vregs for _ in range(3)]
        here = [load(0, 0, v) for v in range(-1, vregs + 1)]
        before = here
        for plane in range(planes):
            after = [load(plane + 1, 0, v) for v in range(-1, vregs + 1)] if plane + 1 < planes else here
            for v in range(vregs):
                value = here[v + 1]
                up = pltpu.roll(jnp.where(bottom, load(plane, -1, v), value), 1, 0)
                down = pltpu.roll(jnp.where(top, load(plane, 1, v), value), SUB - 1, 0)
                left = pltpu.roll(jnp.where(rightmost, here[v], value), 1, 1)
                right = pltpu.roll(jnp.where(leftmost, here[v + 2], value), LANE - 1, 1)
                shade = jnp.tanh(
                    light[0] * (after[v + 1] - before[v + 1]) + light[1] * (down - up) + light[2] * (right - left)
                )
                depth[v] = depth[v] + jnp.log(1.0 + jnp.exp(value + value))
                through = jnp.exp(depth[v] * -scale)
                lost = left_over[v] - through
                left_over[v] = through
                weight = lost + lost * shade
                total[v] = total[v] + weight
                for c in range(3):
                    sums[c][v] = sums[c][v] + weight * jnp.tanh(slope[c] * value + offset[c])
            before, here = here, after
        for v in range(vregs):
            lanes = pl.ds(v * LANE, LANE)
            for c in range(3):
                out_ref[relative, c, pl.ds(out_row, SUB), lanes] = 0.25 * (total[v] + sums[c][v])
            out_ref[relative, 3, pl.ds(out_row, SUB), lanes] = depth[v] * scale

    for k, out_ref in enumerate(out_refs):
        chip = lax.rem(my_chip + k, chips)
        for first, number, low, high, slot, written, before, behind in layout:
            if k == 0:
                for tile in range(low, min(first + 1, high)):
                    tile_copy(tile, slot + tile - low).wait()

            def one_tile(index, carry, k=k, out_ref=out_ref, chip=chip, run=(first, low, high, slot, written, before, behind)):
                first, low, high, slot, written, before, behind = run
                here = slot + first - low + index

                if k == 0:

                    @pl.when(first + index + 1 < high)
                    def _():
                        tile_copy(first + index + 1, here + 1).wait()

                def one(relative, carry):
                    owner = chip * CORES + lax.rem(my_core + relative, CORES)
                    out_row = pl.multiple_of((written + index) * SUB, SUB)
                    march(here, out_row, before, behind, owner * part, relative, out_ref)
                    return carry

                return lax.fori_loop(0, CORES, one, carry)

            lax.fori_loop(0, number, one_tile, 0)


def composite_kernel(chips, where_ref, rank_ref, *refs):
    own, other, out_ref = refs[:chips], refs[chips : 2 * chips], refs[2 * chips]
    my_chip, my_core = where_ref[0], where_ref[1]
    blocks, ranks = [], []
    for k in range(chips):
        chip = lax.rem(my_chip + chips - k, chips)
        for core, ref in ((my_core, own[k]), (CORES - 1 - my_core, other[k])):
            blocks.append(ref)
            ranks.append(rank_ref[chip * CORES + core])
    count = len(blocks)
    ahead = [[(ranks[j] < ranks[i]).astype(jnp.float32) for j in range(count)] for i in range(count)]
    columns = out_ref.shape[2] // LANE

    def one(index, carry):
        row = index // columns
        at = (
            pl.ds(pl.multiple_of(row * SUB, SUB), SUB),
            pl.ds(pl.multiple_of((index - row * columns) * LANE, LANE), LANE),
        )
        depths = [ref[(0, 3, *at)] for ref in blocks]
        sums = [background * jnp.exp(-functools.reduce(jnp.add, depths))] * 3
        for i in range(count):
            front = functools.reduce(jnp.add, [ahead[i][j] * depths[j] for j in range(count) if j != i])
            weight = jnp.exp(-front)
            for c in range(3):
                sums[c] = sums[c] + weight * blocks[i][(0, c, *at)]
        for c in range(3):
            out_ref[(c, *at)] = sums[c]
        return carry

    lax.fori_loop(0, out_ref.shape[1] // SUB * columns, one, 0)


def place_kernel(chips, chunks, where_ref, *refs):
    count = len(chunks) * chips * CORES
    blocks, out_ref, sem = refs[:count], refs[count], refs[count + 1]
    my_chip, my_core = where_ref[0], where_ref[1]
    copies = []
    for i, runs in enumerate(chunks):
        for k in range(chips):
            chip = lax.rem(my_chip + chips - k, chips)
            for j, core in enumerate((my_core, CORES - 1 - my_core)):
                block = blocks[(i * chips + k) * CORES + j]
                part = block.shape[2]
                column = pl.multiple_of((chip * CORES + core) * part, LANE)
                written = 0
                for first, number in runs:
                    copy = pltpu.make_async_copy(
                        block.at[:, pl.ds(written * SUB, number * SUB), :],
                        out_ref.at[:, pl.ds(first * SUB, number * SUB), pl.ds(column, part)],
                        sem.at[len(copies)],
                    )
                    copy.start()
                    copies.append(copy)
                    written += number
    for copy in copies:
        copy.wait()


def body(scalar_field, depth_rank, transfer, light_dir):
    planes, rows, columns = scalar_field.shape
    wide, narrow = lax.axis_size("wide"), lax.axis_size("narrow")
    chips, tiles, part = wide // CORES, rows // SUB, columns // wide
    scale = optical_total / (planes * wide)
    index = lax.axis_index("wide")
    where = jnp.stack([index // CORES, index % CORES]).astype(jnp.int32)
    inner = [(run,) for run in INNER] if tiles == 8 else [((1, tiles - 2),)]
    chunks = inner + [((0, 1), (tiles - 1, 1))]

    smem = pl.BlockSpec(memory_space=pltpu.SMEM)
    vmem = pl.BlockSpec(memory_space=pltpu.VMEM)
    hbm = pl.BlockSpec(memory_space=pltpu.HBM)
    field = pltpu.with_memory_space_constraint(scalar_field, pltpu.HBM)

    def swap(value):
        return lax.ppermute(value, "wide", [(i, i ^ 1) for i in range(wide)])

    def send(value, k):
        return lax.ppermute(value, "wide", [(i, (i + k * CORES) % wide) for i in range(wide)])

    def render(runs, edges=(), events=()):
        slots = sum(min(first + number + 1, tiles) - max(first - 1, 0) for first, number in runs)
        block = pltpu.VMEM((CORES, 4, tiles_of(runs) * SUB, part), jnp.float32)
        return call(
            functools.partial(render_kernel, runs, tiles, chips, scale),
            [where, transfer, light_dir, field, *edges],
            [smem] * 3 + [hbm] + [vmem] * len(edges),
            events,
            out_shape=[block] * chips,
            out_specs=[vmem] * chips,
            scratch_shapes=[
                pltpu.VMEM((planes, slots * SUB, columns + 2 * LANE), jnp.float32),
                pltpu.SemaphoreType.DMA((slots,)),
            ],
            cost_estimate=lasting(2.5 * tiles_of(runs)),
            name="render",
        )

    def edge_rows(events):
        edge = pltpu.VMEM((planes, 1, columns), jnp.float32)
        first_row, last_row = call(
            edges_kernel,
            [field],
            [hbm],
            events,
            out_shape=[edge] * 2,
            out_specs=[vmem] * 2,
            scratch_shapes=[pltpu.VMEM((2, planes, SUB, columns), jnp.float32), pltpu.SemaphoreType.DMA((2,))],
            cost_estimate=lasting(1.2),
            name="edges",
        )
        up = [(i, i + 1) for i in range(narrow - 1)]
        return lax.ppermute(last_row, "narrow", up), lax.ppermute(first_row, "narrow", [(j, i) for i, j in up])

    def composite(runs, own, other, events):
        return call(
            functools.partial(composite_kernel, chips),
            [where, depth_rank, *own, *other],
            [smem] * 2 + [vmem] * (2 * chips),
            events,
            out_shape=pltpu.VMEM((3, tiles_of(runs) * SUB, part), jnp.float32),
            out_specs=vmem,
            cost_estimate=lasting(1.0),
            name="composite",
        )

    sent, last, edges = [], (), ()
    for i, runs in enumerate(chunks):
        if i == len(chunks) - 1:
            edges = edge_rows(last)
        blocks = render(runs, edges, last)
        last = [blocks[0]]
        sent.append([blocks[0]] + [send(blocks[k], k) for k in range(1, chips)])

    finished = []
    for runs, own in zip(chunks, sent):
        other = [swap(value[1:]) for value in own]
        tile = composite(runs, own, other, last)
        last = [tile]
        for k in range(chips):
            value = send(tile, k) if k else tile
            finished += [value, swap(value)]

    return call(
        functools.partial(place_kernel, chips, chunks),
        [where, *finished],
        [smem] + [vmem] * len(finished),
        out_shape=jax.ShapeDtypeStruct((3, rows, columns), jnp.float32),
        out_specs=hbm,
        scratch_shapes=[pltpu.SemaphoreType.DMA((wide * sum(len(runs) for runs in chunks),))],
        cost_estimate=lasting(2.0),
        name="place",
    )


def solution(mesh):
    return jax.shard_map(
        body,
        mesh=mesh,
        in_specs=(P("wide", "narrow", None), P(), P(), P()),
        out_specs=P(None, "narrow", None),
        check_vma=False,
    )
```

```python
import functools

import jax
import jax.numpy as jnp
from jax import lax
from jax.experimental import pallas as pl
from jax.experimental.pallas import tpu as pltpu
from jax.sharding import PartitionSpec as P

background = 0.25
optical_total = 2.0

SUB = 8
LANE = 128
CORES = 2
CHUNKS = (((1, 5),), ((0, 1), (6, 1), (7, 1)))
LOG2E = 1.4426950408889634
VMEM_LIMIT = 24 * 2**20


def call(kernel, operands, specs, events=(), **options):
    def with_events(*refs):
        kernel(*refs[: len(operands)], *refs[len(operands) + len(events) :])

    return pl.pallas_call(
        with_events,
        in_specs=specs + [pl.BlockSpec(memory_space=pl.ANY)] * len(events),
        compiler_params=pltpu.CompilerParams(vmem_limit_bytes=VMEM_LIMIT),
        **options,
    )(*operands, *events)


def lasting(microseconds):
    return pl.CostEstimate(flops=0, bytes_accessed=int(microseconds * 3.69e6), transcendentals=0)


def tiles_of(runs):
    return sum(number for _, number in runs)


def edges_kernel(field_ref, first_ref, last_ref, buffer, sem):
    rows = field_ref.shape[1]
    copies = [
        pltpu.make_async_copy(field_ref.at[:, pl.ds(row, SUB), :], buffer.at[i], sem.at[i])
        for i, row in enumerate((0, rows - SUB))
    ]
    for copy in copies:
        copy.start()
    for copy in copies:
        copy.wait()
    first_ref[...] = buffer[0, :, :1, :]
    last_ref[...] = buffer[1, :, SUB - 1 :, :]


def render_kernel(runs, tiles, chips, scale, where_ref, transfer_ref, light_ref, field_ref, *refs):
    out_refs, (padded, sem) = refs[-2 - chips : -2], refs[-2:]
    edges = list(refs[: -2 - chips])
    planes, _, columns = field_ref.shape
    part = out_refs[0].shape[3]
    my_chip, my_core = where_ref[0], where_ref[1]

    def tile_copy(tile, slot):
        return pltpu.make_async_copy(
            field_ref.at[:, pl.ds(pl.multiple_of(tile * SUB, SUB), SUB), :],
            padded.at[:, pl.ds(pl.multiple_of(slot * SUB, SUB), SUB), pl.ds(LANE, columns)],
            sem.at[slot],
        )

    layout, slot, written = [], 0, 0
    for first, number in runs:
        low, high = max(first - 1, 0), min(first + number + 1, tiles)
        before = edges.pop(0) if first == 0 else None
        behind = edges.pop(0) if first + number == tiles else None
        layout.append((first, number, low, high, slot, written, before, behind))
        for tile in range(low, high):
            tile_copy(tile, slot + tile - low).start()
        slot, written = slot + high - low, written + number
    rim = jnp.zeros((planes, padded.shape[1], LANE), jnp.float32)
    padded[:, :, :LANE] = rim
    padded[:, :, LANE + columns :] = rim

    light = [0.5 * light_ref[i] for i in range(3)]
    slope = [0.5 * transfer_ref[0, c] for c in range(3)]
    offset = [0.5 * transfer_ref[1, c] for c in range(3)]
    sub = lax.broadcasted_iota(jnp.int32, (SUB, LANE), 0)
    lane = lax.broadcasted_iota(jnp.int32, (SUB, LANE), 1)
    top, bottom = sub == 0, sub == SUB - 1
    leftmost, rightmost = lane == 0, lane == LANE - 1
    vregs = CORES * part // LANE

    def march(slot, out_row, before_ref, behind_ref, column, out_ref):
        def load(plane, shift, vreg):
            ref = {-1: before_ref, 1: behind_ref}.get(shift)
            if ref is not None:
                lanes = pl.ds(pl.multiple_of(column + vreg * LANE, LANE), LANE)
                return jnp.broadcast_to(ref[plane, :, lanes], (SUB, LANE))
            return padded[
                plane,
                pl.ds(pl.multiple_of((slot + shift) * SUB, SUB), SUB),
                pl.ds(pl.multiple_of(column + (1 + vreg) * LANE, LANE), LANE),
            ]

        zero = jnp.zeros((SUB, LANE), jnp.float32)
        depth = [zero] * vregs
        left_over = [zero + 1.0] * vregs
        total = [zero] * vregs
        sums = [[zero] * vregs for _ in range(3)]
        here = [load(0, 0, v) for v in range(-1, vregs + 1)]
        before = here
        for plane in range(planes):
            after = [load(plane + 1, 0, v) for v in range(-1, vregs + 1)] if plane + 1 < planes else here
            for v in range(vregs):
                value = here[v + 1]
                up = pltpu.roll(jnp.where(bottom, load(plane, -1, v), value), 1, 0)
                down = pltpu.roll(jnp.where(top, load(plane, 1, v), value), SUB - 1, 0)
                left = pltpu.roll(jnp.where(rightmost, here[v], value), 1, 1)
                right = pltpu.roll(jnp.where(leftmost, here[v + 2], value), LANE - 1, 1)
                shade = jnp.tanh(
                    light[0] * (after[v + 1] - before[v + 1]) + light[1] * (down - up) + light[2] * (right - left)
                )
                depth[v] = depth[v] + jnp.log2(1.0 + jnp.exp2(value * (2.0 * LOG2E)))
                through = jnp.exp2(depth[v] * -scale)
                lost = left_over[v] - through
                left_over[v] = through
                weight = lost + lost * shade
                total[v] = total[v] + weight
                for c in range(3):
                    sums[c][v] = sums[c][v] + weight * jnp.tanh(slope[c] * value + offset[c])
            before, here = here, after
        for v in range(vregs):
            relative = lax.rem(my_core + v * LANE // part, CORES)
            lanes = pl.ds(v * LANE % part, LANE)
            for c in range(3):
                out_ref[relative, c, pl.ds(out_row, SUB), lanes] = 0.25 * (total[v] + sums[c][v])
            out_ref[relative, 3, pl.ds(out_row, SUB), lanes] = depth[v] * scale

    for k, out_ref in enumerate(out_refs):
        chip = lax.rem(my_chip + k, chips)
        for first, number, low, high, slot, written, before, behind in layout:
            if k == 0:
                for tile in range(low, min(first + 1, high)):
                    tile_copy(tile, slot + tile - low).wait()

            def one_tile(index, carry, k=k, out_ref=out_ref, chip=chip, run=(first, low, high, slot, written, before, behind)):
                first, low, high, slot, written, before, behind = run
                here = slot + first - low + index

                if k == 0:

                    @pl.when(first + index + 1 < high)
                    def _():
                        tile_copy(first + index + 1, here + 1).wait()

                out_row = pl.multiple_of((written + index) * SUB, SUB)
                march(here, out_row, before, behind, pl.multiple_of(chip * CORES * part, LANE), out_ref)
                return carry

            lax.fori_loop(0, number, one_tile, 0)


def composite_kernel(chips, count, where_ref, rank_ref, *refs):
    inputs, out_ref = refs[:-1], refs[-1]
    my_chip, my_core = where_ref[0], where_ref[1]
    ranks = []
    for k in range(chips):
        chip = lax.rem(my_chip + chips - k, chips)
        ranks += [rank_ref[chip * CORES + core] for core in (my_core, CORES - 1 - my_core)]
    bricks = len(ranks)
    ahead = [[(ranks[j] < ranks[i]).astype(jnp.float32) for j in range(bricks)] for i in range(bricks)]
    columns = out_ref.shape[2] // LANE
    written = 0
    for n in range(count):
        own, other = inputs[2 * n * chips : (2 * n + 1) * chips], inputs[(2 * n + 1) * chips : (2 * n + 2) * chips]
        blocks = [ref for pair in zip(own, other) for ref in pair]
        rows = own[0].shape[2]

        def one(index, carry, blocks=blocks, written=written):
            tile = index // columns
            row = pl.multiple_of(tile * SUB, SUB)
            lanes = pl.ds(pl.multiple_of((index - tile * columns) * LANE, LANE), LANE)
            at = (pl.ds(row, SUB), lanes)
            depths = [ref[(0, 3, *at)] for ref in blocks]
            sums = [background * jnp.exp2(-functools.reduce(jnp.add, depths))] * 3
            for i in range(bricks):
                front = functools.reduce(jnp.add, [ahead[i][j] * depths[j] for j in range(bricks) if j != i])
                weight = jnp.exp2(-front)
                for c in range(3):
                    sums[c] = sums[c] + weight * blocks[i][(0, c, *at)]
            for c in range(3):
                out_ref[c, pl.ds(pl.multiple_of(row + written, SUB), SUB), lanes] = sums[c]
            return carry

        lax.fori_loop(0, rows // SUB * columns, one, 0)
        written += rows


def place_kernel(groups, where_ref, *refs):
    blocks, out_ref, sem = list(refs[:-2]), refs[-2], refs[-1]
    my_chip, my_core = where_ref[0], where_ref[1]
    copies = []
    for runs, chip_of in groups:
        for chip in chip_of(my_chip):
            for core in (my_core, CORES - 1 - my_core):
                block = blocks.pop(0)
                part = block.shape[2]
                column = pl.multiple_of((chip * CORES + core) * part, LANE)
                written = 0
                for first, number in runs:
                    copy = pltpu.make_async_copy(
                        block.at[:, pl.ds(written * SUB, number * SUB), :],
                        out_ref.at[:, pl.ds(first * SUB, number * SUB), pl.ds(column, part)],
                        sem.at[len(copies)],
                    )
                    copy.start()
                    copies.append(copy)
                    written += number
    for copy in copies:
        copy.wait()


def body(scalar_field, depth_rank, transfer, light_dir):
    planes, rows, columns = scalar_field.shape
    wide, narrow = lax.axis_size("wide"), lax.axis_size("narrow")
    chips, tiles, part = wide // CORES, rows // SUB, columns // wide
    scale = optical_total / (planes * wide)
    index = lax.axis_index("wide")
    where = jnp.stack([index // CORES, index % CORES]).astype(jnp.int32)
    chunks = CHUNKS if tiles == 8 else (((1, tiles - 2),), ((0, 1), (tiles - 1, 1)))

    smem = pl.BlockSpec(memory_space=pltpu.SMEM)
    vmem = pl.BlockSpec(memory_space=pltpu.VMEM)
    hbm = pl.BlockSpec(memory_space=pltpu.HBM)
    field = pltpu.with_memory_space_constraint(scalar_field, pltpu.HBM)

    def swap(value):
        return lax.ppermute(value, "wide", [(i, i ^ 1) for i in range(wide)])

    def send(value, k):
        return lax.ppermute(value, "wide", [(i, (i + k * CORES) % wide) for i in range(wide)])

    def render(runs, edges=(), events=()):
        slots = sum(min(first + number + 1, tiles) - max(first - 1, 0) for first, number in runs)
        block = pltpu.VMEM((CORES, 4, tiles_of(runs) * SUB, part), jnp.float32)
        return call(
            functools.partial(render_kernel, runs, tiles, chips, scale),
            [where, transfer, light_dir, field, *edges],
            [smem] * 3 + [hbm] + [vmem] * len(edges),
            events,
            out_shape=[block] * chips,
            out_specs=[vmem] * chips,
            scratch_shapes=[
                pltpu.VMEM((planes, slots * SUB, columns + 2 * LANE), jnp.float32),
                pltpu.SemaphoreType.DMA((slots,)),
            ],
            cost_estimate=lasting(2.5 * tiles_of(runs)),
            name="render",
        )

    def edge_rows(events):
        edge = pltpu.VMEM((planes, 1, columns), jnp.float32)
        first_row, last_row = call(
            edges_kernel,
            [field],
            [hbm],
            events,
            out_shape=[edge] * 2,
            out_specs=[vmem] * 2,
            scratch_shapes=[pltpu.VMEM((2, planes, SUB, columns), jnp.float32), pltpu.SemaphoreType.DMA((2,))],
            cost_estimate=lasting(1.2),
            name="edges",
        )
        up = [(i, i + 1) for i in range(narrow - 1)]
        return lax.ppermute(last_row, "narrow", up), lax.ppermute(first_row, "narrow", [(j, i) for i, j in up])

    def composite(parts_of, runs, events):
        operands = []
        for own in parts_of:
            operands += own + [swap(value[1:]) for value in own]
        return call(
            functools.partial(composite_kernel, chips, len(parts_of)),
            [where, depth_rank, *operands],
            [smem] * 2 + [vmem] * len(operands),
            events,
            out_shape=pltpu.VMEM((3, tiles_of(runs) * SUB, part), jnp.float32),
            out_specs=vmem,
            cost_estimate=lasting(1.0),
            name="composite",
        )

    def gather_by_halves(tile):
        tiles_by = {0: tile}
        bit = chips // 2
        while bit:
            for m in list(tiles_by):
                pairs = [(i, i ^ (bit * CORES)) for i in range(wide)]
                tiles_by[m ^ bit] = lax.ppermute(tiles_by[m], "wide", pairs)
            bit //= 2
        order = sorted(tiles_by)
        return [tiles_by[m] for m in order], lambda chip: [jnp.bitwise_xor(chip, m) for m in order]

    def gather_directly(tile):
        values = [tile] + [send(tile, k) for k in range(1, chips)]
        return values, lambda chip: [lax.rem(chip + chips - k, chips) for k in range(chips)]

    sent, last, edges = [], [], ()
    for i, runs in enumerate(chunks):
        if i == len(chunks) - 1:
            edges = edge_rows(last)
        blocks = render(runs, edges, last)
        last = [blocks[0]]
        sent.append([blocks[0]] + [send(blocks[k], k) for k in range(1, chips)])

    groups, finished = [], []
    for first, end, gather in ((0, len(chunks) - 1, gather_by_halves), (len(chunks) - 1, len(chunks), gather_directly)):
        runs = sum(chunks[first:end], ())
        tile = composite(sent[first:end], runs, last)
        last = [tile]
        values, chip_of = gather(tile)
        groups.append((runs, chip_of))
        for value in values:
            finished += [value, swap(value)]

    return call(
        functools.partial(place_kernel, groups),
        [where, *finished],
        [smem] + [vmem] * len(finished),
        out_shape=jax.ShapeDtypeStruct((3, rows, columns), jnp.float32),
        out_specs=hbm,
        scratch_shapes=[pltpu.SemaphoreType.DMA((wide * sum(len(runs) for runs, _ in groups),))],
        cost_estimate=lasting(2.0),
        name="place",
    )


def solution(mesh):
    return jax.shard_map(
        body,
        mesh=mesh,
        in_specs=(P("wide", "narrow", None), P(), P(), P()),
        out_specs=P(None, "narrow", None),
        check_vma=False,
    )
```

```python
import functools

import jax
import jax.numpy as jnp
from jax import lax
from jax.experimental import pallas as pl
from jax.experimental.pallas import tpu as pltpu
from jax.sharding import PartitionSpec as P

background = 0.25
optical_total = 2.0

SUB = 8
LANE = 128
CORES = 2
CHUNKS = (((1, 5),), ((0, 1), (6, 1), (7, 1)))
LOG2E = 1.4426950408889634
VMEM_LIMIT = 24 * 2**20


def call(kernel, operands, specs, events=(), **options):
    def with_events(*refs):
        kernel(*refs[: len(operands)], *refs[len(operands) + len(events) :])

    return pl.pallas_call(
        with_events,
        in_specs=list(specs) + [pl.BlockSpec(memory_space=pl.ANY)] * len(events),
        compiler_params=pltpu.CompilerParams(vmem_limit_bytes=VMEM_LIMIT),
        **options,
    )(*operands, *events)


def lasting(microseconds):
    return pl.CostEstimate(flops=0, bytes_accessed=int(microseconds * 3.69e6), transcendentals=0)


def tiles_of(runs):
    return sum(number for _, number in runs)


def edges_kernel(field_ref, first_ref, last_ref, sem):
    rows = field_ref.shape[1]
    copies = [
        pltpu.make_async_copy(field_ref.at[:, pl.ds(row, 1), :], ref, sem.at[i])
        for i, (row, ref) in enumerate(((0, first_ref), (rows - 1, last_ref)))
    ]
    for copy in copies:
        copy.start()
    for copy in copies:
        copy.wait()


def render_kernel(runs, tiles, chips, offsets, scale, where_ref, transfer_ref, light_ref, field_ref, *refs):
    out_refs, (padded, sem) = refs[-2 - len(offsets) : -2], refs[-2:]
    edges = list(refs[: -2 - len(offsets)])
    planes, _, columns = field_ref.shape
    part = out_refs[0].shape[3]
    my_chip, my_core = where_ref[0], where_ref[1]

    def tile_copy(tile, slot):
        return pltpu.make_async_copy(
            field_ref.at[:, pl.ds(pl.multiple_of(tile * SUB, SUB), SUB), :],
            padded.at[:, pl.ds(pl.multiple_of(slot * SUB, SUB), SUB), pl.ds(LANE, columns)],
            sem.at[slot],
        )

    layout, slot, written = [], 0, 0
    for first, number in runs:
        low, high = max(first - 1, 0), min(first + number + 1, tiles)
        before = edges.pop(0) if first == 0 else None
        behind = edges.pop(0) if first + number == tiles else None
        layout.append((first, number, low, high, slot, written, before, behind))
        for tile in range(low, high):
            tile_copy(tile, slot + tile - low).start()
        slot, written = slot + high - low, written + number
    rim = jnp.zeros((planes, padded.shape[1], LANE), jnp.float32)
    padded[:, :, :LANE] = rim
    padded[:, :, LANE + columns :] = rim

    light = [0.5 * light_ref[i] for i in range(3)]
    slope = [0.5 * transfer_ref[0, c] for c in range(3)]
    offset = [0.5 * transfer_ref[1, c] for c in range(3)]
    sub = lax.broadcasted_iota(jnp.int32, (SUB, LANE), 0)
    lane = lax.broadcasted_iota(jnp.int32, (SUB, LANE), 1)
    top, bottom = sub == 0, sub == SUB - 1
    leftmost, rightmost = lane == 0, lane == LANE - 1
    vregs = CORES * part // LANE

    def march(slot, out_row, before_ref, behind_ref, column, out_ref):
        def load(plane, shift, vreg):
            ref = {-1: before_ref, 1: behind_ref}.get(shift)
            if ref is not None:
                lanes = pl.ds(pl.multiple_of(column + vreg * LANE, LANE), LANE)
                return jnp.broadcast_to(ref[plane, :, lanes], (SUB, LANE))
            return padded[
                plane,
                pl.ds(pl.multiple_of((slot + shift) * SUB, SUB), SUB),
                pl.ds(pl.multiple_of(column + (1 + vreg) * LANE, LANE), LANE),
            ]

        zero = jnp.zeros((SUB, LANE), jnp.float32)
        depth = [zero] * vregs
        left_over = [zero + 1.0] * vregs
        total = [zero] * vregs
        sums = [[zero] * vregs for _ in range(3)]
        here = [load(0, 0, v) for v in range(-1, vregs + 1)]
        before = here
        for plane in range(planes):
            after = [load(plane + 1, 0, v) for v in range(-1, vregs + 1)] if plane + 1 < planes else here
            for v in range(vregs):
                value = here[v + 1]
                up = pltpu.roll(jnp.where(bottom, load(plane, -1, v), value), 1, 0)
                down = pltpu.roll(jnp.where(top, load(plane, 1, v), value), SUB - 1, 0)
                left = pltpu.roll(jnp.where(rightmost, here[v], value), 1, 1)
                right = pltpu.roll(jnp.where(leftmost, here[v + 2], value), LANE - 1, 1)
                shade = jnp.tanh(
                    light[0] * (after[v + 1] - before[v + 1]) + light[1] * (down - up) + light[2] * (right - left)
                )
                depth[v] = depth[v] + jnp.log2(1.0 + jnp.exp2(value * (2.0 * LOG2E)))
                through = jnp.exp2(depth[v] * -scale)
                lost = left_over[v] - through
                left_over[v] = through
                weight = lost + lost * shade
                total[v] = total[v] + weight
                for c in range(3):
                    sums[c][v] = sums[c][v] + weight * jnp.tanh(slope[c] * value + offset[c])
            before, here = here, after
        for v in range(vregs):
            relative = lax.rem(my_core + v * LANE // part, CORES)
            lanes = pl.ds(v * LANE % part, LANE)
            for c in range(3):
                out_ref[relative, c, pl.ds(out_row, SUB), lanes] = 0.25 * (total[v] + sums[c][v])
            out_ref[relative, 3, pl.ds(out_row, SUB), lanes] = depth[v] * scale

    for step, (k, out_ref) in enumerate(zip(offsets, out_refs)):
        chip = lax.rem(my_chip + k, chips)
        for first, number, low, high, slot, written, before, behind in layout:
            if step == 0:
                for tile in range(low, min(first + 1, high)):
                    tile_copy(tile, slot + tile - low).wait()

            def one_tile(index, carry, step=step, out_ref=out_ref, chip=chip, run=(first, low, high, slot, written, before, behind)):
                first, low, high, slot, written, before, behind = run
                here = slot + first - low + index

                if step == 0:

                    @pl.when(first + index + 1 < high)
                    def _():
                        tile_copy(first + index + 1, here + 1).wait()

                out_row = pl.multiple_of((written + index) * SUB, SUB)
                march(here, out_row, before, behind, pl.multiple_of(chip * CORES * part, LANE), out_ref)
                return carry

            lax.fori_loop(0, number, one_tile, 0)


def split_kernel(*refs):
    count = len(refs) // 2
    for block_ref, out_ref in zip(refs[:count], refs[count:]):
        out_ref[...] = block_ref[1:]


def composite_kernel(chips, where_ref, rank_ref, *refs):
    own, other, out_ref = refs[:chips], refs[chips:-1], refs[-1]
    my_chip, my_core = where_ref[0], where_ref[1]
    blocks, ranks = [], []
    for k in range(chips):
        chip = lax.rem(my_chip + chips - k, chips)
        for core, ref in ((my_core, own[k]), (CORES - 1 - my_core, other[k])):
            blocks.append(ref)
            ranks.append(rank_ref[chip * CORES + core])
    bricks = len(ranks)
    ahead = [[(ranks[j] < ranks[i]).astype(jnp.float32) for j in range(bricks)] for i in range(bricks)]
    columns = out_ref.shape[2] // LANE

    def one(index, carry):
        tile = index // columns
        lanes = pl.ds(pl.multiple_of((index - tile * columns) * LANE, LANE), LANE)
        at = (pl.ds(pl.multiple_of(tile * SUB, SUB), SUB), lanes)
        depths = [ref[(0, 3, *at)] for ref in blocks]
        sums = [background * jnp.exp2(-functools.reduce(jnp.add, depths))] * 3
        for i in range(bricks):
            front = functools.reduce(jnp.add, [ahead[i][j] * depths[j] for j in range(bricks) if j != i])
            weight = jnp.exp2(-front)
            for c in range(3):
                sums[c] = sums[c] + weight * blocks[i][(0, c, *at)]
        for c in range(3):
            out_ref[(c, *at)] = sums[c]
        return carry

    lax.fori_loop(0, out_ref.shape[1] // SUB * columns, one, 0)


def place_kernel(groups, where_ref, *refs):
    blocks, out_ref, sem = list(refs[:-2]), refs[-2], refs[-1]
    my_chip, my_core = where_ref[0], where_ref[1]
    copies = []
    for runs, chip_of in groups:
        for chip in chip_of(my_chip):
            for core in (my_core, CORES - 1 - my_core):
                block = blocks.pop(0)
                part = block.shape[2]
                column = pl.multiple_of((chip * CORES + core) * part, LANE)
                written = 0
                for first, number in runs:
                    copy = pltpu.make_async_copy(
                        block.at[:, pl.ds(written * SUB, number * SUB), :],
                        out_ref.at[:, pl.ds(first * SUB, number * SUB), pl.ds(column, part)],
                        sem.at[len(copies)],
                    )
                    copy.start()
                    copies.append(copy)
                    written += number
    for copy in copies:
        copy.wait()


def body(scalar_field, depth_rank, transfer, light_dir):
    planes, rows, columns = scalar_field.shape
    wide, narrow = lax.axis_size("wide"), lax.axis_size("narrow")
    chips, tiles, part = wide // CORES, rows // SUB, columns // wide
    scale = optical_total / (planes * wide)
    index = lax.axis_index("wide")
    where = jnp.stack([index // CORES, index % CORES]).astype(jnp.int32)
    chunks = CHUNKS if tiles == 8 else (((1, tiles - 2),), ((0, 1), (tiles - 1, 1)))

    smem = pl.BlockSpec(memory_space=pltpu.SMEM)
    vmem = pl.BlockSpec(memory_space=pltpu.VMEM)
    hbm = pl.BlockSpec(memory_space=pltpu.HBM)
    field = pltpu.with_memory_space_constraint(scalar_field, pltpu.HBM)

    def swap(value):
        return lax.ppermute(value, "wide", [(i, i ^ 1) for i in range(wide)])

    def send(value, k):
        return lax.ppermute(value, "wide", [(i, (i + k * CORES) % wide) for i in range(wide)])

    def render(runs, offsets, edges, events):
        slots = sum(min(first + number + 1, tiles) - max(first - 1, 0) for first, number in runs)
        block = pltpu.VMEM((CORES, 4, tiles_of(runs) * SUB, part), jnp.float32)
        return call(
            functools.partial(render_kernel, runs, tiles, chips, offsets, scale),
            [where, transfer, light_dir, field, *edges],
            [smem] * 3 + [hbm] + [vmem] * len(edges),
            events,
            out_shape=[block] * len(offsets),
            out_specs=[vmem] * len(offsets),
            scratch_shapes=[
                pltpu.VMEM((planes, slots * SUB, columns + 2 * LANE), jnp.float32),
                pltpu.SemaphoreType.DMA((slots,)),
            ],
            cost_estimate=lasting(0.6 * len(offsets) * tiles_of(runs)),
            name="render",
        )

    def edge_rows(events):
        edge = pltpu.VMEM((planes, 1, columns), jnp.float32)
        first_row, last_row = call(
            edges_kernel,
            [field],
            [hbm],
            events,
            out_shape=[edge] * 2,
            out_specs=[vmem] * 2,
            scratch_shapes=[pltpu.SemaphoreType.DMA((2,))],
            cost_estimate=lasting(1.2),
            name="edges",
        )
        up = [(i, i + 1) for i in range(narrow - 1)]
        return lax.ppermute(last_row, "narrow", up), lax.ppermute(first_row, "narrow", [(j, i) for i, j in up])

    def other_halves(arrays, events):
        halves = call(
            split_kernel,
            arrays,
            [vmem] * len(arrays),
            events,
            out_shape=[pltpu.VMEM((1, *arrays[0].shape[1:]), jnp.float32)] * len(arrays),
            out_specs=[vmem] * len(arrays),
            cost_estimate=lasting(0.3),
            name="split",
        )
        return [swap(value) for value in halves]

    def composite(own, other, runs):
        return call(
            functools.partial(composite_kernel, chips),
            [where, depth_rank, *own, *other],
            [smem] * 2 + [vmem] * (2 * chips),
            out_shape=pltpu.VMEM((3, tiles_of(runs) * SUB, part), jnp.float32),
            out_specs=vmem,
            cost_estimate=lasting(1.0),
            name="composite",
        )

    def gather_by_halves(tile):
        tiles_by = {0: tile}
        bit = chips // 2
        while bit:
            for m in list(tiles_by):
                pairs = [(i, i ^ (bit * CORES)) for i in range(wide)]
                tiles_by[m ^ bit] = lax.ppermute(tiles_by[m], "wide", pairs)
            bit //= 2
        order = sorted(tiles_by)
        return [tiles_by[m] for m in order], lambda chip: [jnp.bitwise_xor(chip, m) for m in order]

    def gather_directly(tile):
        values = [tile] + [send(tile, k) for k in range(1, chips)]
        return values, lambda chip: [lax.rem(chip + chips - k, chips) for k in range(chips)]

    early = [tuple(range(chips // 2, 0, -1)), (*range(chips // 2 + 1, chips), 0)]
    sent, near, last, edges = [], [], [], ()
    for i, runs in enumerate(chunks):
        if i == len(chunks) - 1:
            edges = edge_rows(last)
        blocks = {}
        for offsets in early if i == 0 else [tuple(range(chips))]:
            values = render(runs, offsets, edges, last)
            blocks.update(zip(offsets, values))
            last = list(values[:1])
        near += other_halves([blocks[0]], [])
        sent.append([blocks[0]] + [send(blocks[k], k) for k in range(1, chips)])

    groups, finished = [], []
    for runs, own, first, gather in zip(chunks, sent, near, (gather_by_halves, gather_directly)):
        other = [first] + other_halves(own[1:], last)
        tile = composite(own, other, runs)
        values, chip_of = gather(tile)
        last = values[2:3]
        groups.append((runs, chip_of))
        for value in values:
            finished += [value, swap(value)]

    return call(
        functools.partial(place_kernel, groups),
        [where, *finished],
        [smem] + [vmem] * len(finished),
        out_shape=jax.ShapeDtypeStruct((3, rows, columns), jnp.float32),
        out_specs=hbm,
        scratch_shapes=[pltpu.SemaphoreType.DMA((wide * sum(len(runs) for runs, _ in groups),))],
        cost_estimate=lasting(2.0),
        name="place",
    )


def solution(mesh):
    return jax.shard_map(
        body,
        mesh=mesh,
        in_specs=(P("wide", "narrow", None), P(), P(), P()),
        out_specs=P(None, "narrow", None),
        check_vma=False,
    )
```

```python
import functools

import jax
import jax.numpy as jnp
from jax import lax
from jax.experimental import pallas as pl
from jax.experimental.pallas import tpu as pltpu
from jax.sharding import PartitionSpec as P

background = 0.25
optical_total = 2.0

SUB = 8
LANE = 128
CORES = 2
CHUNKS = (((1, 5),), ((0, 1), (6, 1), (7, 1)))
LOG2E = 1.4426950408889634
VMEM_LIMIT = 24 * 2**20


def call(kernel, operands, specs, events=(), **options):
    def with_events(*refs):
        kernel(*refs[: len(operands)], *refs[len(operands) + len(events) :])

    return pl.pallas_call(
        with_events,
        in_specs=list(specs) + [pl.BlockSpec(memory_space=pl.ANY)] * len(events),
        compiler_params=pltpu.CompilerParams(vmem_limit_bytes=VMEM_LIMIT),
        **options,
    )(*operands, *events)


def lasting(microseconds):
    return pl.CostEstimate(flops=0, bytes_accessed=int(microseconds * 3.69e6), transcendentals=0)


def tiles_of(runs):
    return sum(number for _, number in runs)


def edges_kernel(field_ref, first_ref, last_ref, sem):
    rows = field_ref.shape[1]
    copies = [
        pltpu.make_async_copy(field_ref.at[:, pl.ds(row, 1), :], ref, sem.at[i])
        for i, (row, ref) in enumerate(((0, first_ref), (rows - 1, last_ref)))
    ]
    for copy in copies:
        copy.start()
    for copy in copies:
        copy.wait()


def render_kernel(runs, tiles, chips, offsets, scale, given, where_ref, transfer_ref, light_ref, field_ref, *refs):
    if given:
        edges, padded, out_refs, sem = [], refs[0], refs[1:-1], refs[-1]
    else:
        out_refs, (padded, sem) = refs[-2 - len(offsets) : -2], refs[-2:]
        edges = list(refs[: -2 - len(offsets)])
    planes, _, columns = field_ref.shape
    part = out_refs[0].shape[3]
    my_chip, my_core = where_ref[0], where_ref[1]

    def tile_copy(tile, slot):
        return pltpu.make_async_copy(
            field_ref.at[:, pl.ds(pl.multiple_of(tile * SUB, SUB), SUB), :],
            padded.at[:, pl.ds(pl.multiple_of(slot * SUB, SUB), SUB), pl.ds(LANE, columns)],
            sem.at[slot],
        )

    layout, slot, written = [], 0, 0
    for first, number in runs:
        low, high = max(first - 1, 0), min(first + number + 1, tiles)
        before = edges.pop(0) if first == 0 else None
        behind = edges.pop(0) if first + number == tiles else None
        layout.append((first, number, low, high, slot, written, before, behind))
        for tile in range(low, high) if not given else ():
            tile_copy(tile, slot + tile - low).start()
        slot, written = slot + high - low, written + number
    if not given:
        rim = jnp.zeros((planes, padded.shape[1], LANE), jnp.float32)
        padded[:, :, :LANE] = rim
        padded[:, :, LANE + columns :] = rim

    light = [0.5 * light_ref[i] for i in range(3)]
    slope = [0.5 * transfer_ref[0, c] for c in range(3)]
    offset = [0.5 * transfer_ref[1, c] for c in range(3)]
    sub = lax.broadcasted_iota(jnp.int32, (SUB, LANE), 0)
    lane = lax.broadcasted_iota(jnp.int32, (SUB, LANE), 1)
    top, bottom = sub == 0, sub == SUB - 1
    leftmost, rightmost = lane == 0, lane == LANE - 1
    vregs = CORES * part // LANE

    def march(slot, out_row, before_ref, behind_ref, column, out_ref):
        def load(plane, shift, vreg):
            ref = {-1: before_ref, 1: behind_ref}.get(shift)
            if ref is not None:
                lanes = pl.ds(pl.multiple_of(column + vreg * LANE, LANE), LANE)
                return jnp.broadcast_to(ref[plane, :, lanes], (SUB, LANE))
            return padded[
                plane,
                pl.ds(pl.multiple_of((slot + shift) * SUB, SUB), SUB),
                pl.ds(pl.multiple_of(column + (1 + vreg) * LANE, LANE), LANE),
            ]

        zero = jnp.zeros((SUB, LANE), jnp.float32)
        depth = [zero] * vregs
        left_over = [zero + 1.0] * vregs
        total = [zero] * vregs
        sums = [[zero] * vregs for _ in range(3)]
        here = [load(0, 0, v) for v in range(-1, vregs + 1)]
        before = here
        for plane in range(planes):
            after = [load(plane + 1, 0, v) for v in range(-1, vregs + 1)] if plane + 1 < planes else here
            for v in range(vregs):
                value = here[v + 1]
                up = pltpu.roll(jnp.where(bottom, load(plane, -1, v), value), 1, 0)
                down = pltpu.roll(jnp.where(top, load(plane, 1, v), value), SUB - 1, 0)
                left = pltpu.roll(jnp.where(rightmost, here[v], value), 1, 1)
                right = pltpu.roll(jnp.where(leftmost, here[v + 2], value), LANE - 1, 1)
                shade = jnp.tanh(
                    light[0] * (after[v + 1] - before[v + 1]) + light[1] * (down - up) + light[2] * (right - left)
                )
                depth[v] = depth[v] + jnp.log2(1.0 + jnp.exp2(value * (2.0 * LOG2E)))
                through = jnp.exp2(depth[v] * -scale)
                lost = left_over[v] - through
                left_over[v] = through
                weight = lost + lost * shade
                total[v] = total[v] + weight
                for c in range(3):
                    sums[c][v] = sums[c][v] + weight * jnp.tanh(slope[c] * value + offset[c])
            before, here = here, after
        for v in range(vregs):
            relative = lax.rem(my_core + v * LANE // part, CORES)
            lanes = pl.ds(v * LANE % part, LANE)
            for c in range(3):
                out_ref[relative, c, pl.ds(out_row, SUB), lanes] = 0.25 * (total[v] + sums[c][v])
            out_ref[relative, 3, pl.ds(out_row, SUB), lanes] = depth[v] * scale

    for step, (k, out_ref) in enumerate(zip(offsets, out_refs)):
        chip = lax.rem(my_chip + k, chips)
        for first, number, low, high, slot, written, before, behind in layout:
            if step == 0 and not given:
                for tile in range(low, min(first + 1, high)):
                    tile_copy(tile, slot + tile - low).wait()

            def one_tile(index, carry, step=step, out_ref=out_ref, chip=chip, run=(first, low, high, slot, written, before, behind)):
                first, low, high, slot, written, before, behind = run
                here = slot + first - low + index

                if step == 0 and not given:

                    @pl.when(first + index + 1 < high)
                    def _():
                        tile_copy(first + index + 1, here + 1).wait()

                out_row = pl.multiple_of((written + index) * SUB, SUB)
                march(here, out_row, before, behind, pl.multiple_of(chip * CORES * part, LANE), out_ref)
                return carry

            lax.fori_loop(0, number, one_tile, 0)


def relay_kernel(*refs):
    del refs


def split_kernel(*refs):
    count = len(refs) // 2
    for block_ref, out_ref in zip(refs[:count], refs[count:]):
        out_ref[...] = block_ref[1:]


def composite_kernel(chips, where_ref, rank_ref, *refs):
    own, other, out_ref = refs[:chips], refs[chips:-1], refs[-1]
    my_chip, my_core = where_ref[0], where_ref[1]
    blocks, ranks = [], []
    for k in range(chips):
        chip = lax.rem(my_chip + chips - k, chips)
        for core, ref in ((my_core, own[k]), (CORES - 1 - my_core, other[k])):
            blocks.append(ref)
            ranks.append(rank_ref[chip * CORES + core])
    bricks = len(ranks)
    ahead = [[(ranks[j] < ranks[i]).astype(jnp.float32) for j in range(bricks)] for i in range(bricks)]
    columns = out_ref.shape[2] // LANE

    def one(index, carry):
        tile = index // columns
        lanes = pl.ds(pl.multiple_of((index - tile * columns) * LANE, LANE), LANE)
        at = (pl.ds(pl.multiple_of(tile * SUB, SUB), SUB), lanes)
        depths = [ref[(0, 3, *at)] for ref in blocks]
        sums = [background * jnp.exp2(-functools.reduce(jnp.add, depths))] * 3
        for i in range(bricks):
            front = functools.reduce(jnp.add, [ahead[i][j] * depths[j] for j in range(bricks) if j != i])
            weight = jnp.exp2(-front)
            for c in range(3):
                sums[c] = sums[c] + weight * blocks[i][(0, c, *at)]
        for c in range(3):
            out_ref[(c, *at)] = sums[c]
        return carry

    lax.fori_loop(0, out_ref.shape[1] // SUB * columns, one, 0)


def place_kernel(groups, where_ref, *refs):
    blocks, out_ref, sem = list(refs[:-2]), refs[-2], refs[-1]
    my_chip, my_core = where_ref[0], where_ref[1]
    copies = []
    for runs, chip_of in groups:
        for chip in chip_of(my_chip):
            for core in (my_core, CORES - 1 - my_core):
                block = blocks.pop(0)
                part = block.shape[2]
                column = pl.multiple_of((chip * CORES + core) * part, LANE)
                written = 0
                for first, number in runs:
                    copy = pltpu.make_async_copy(
                        block.at[:, pl.ds(written * SUB, number * SUB), :],
                        out_ref.at[:, pl.ds(first * SUB, number * SUB), pl.ds(column, part)],
                        sem.at[len(copies)],
                    )
                    copy.start()
                    copies.append(copy)
                    written += number
    for copy in copies:
        copy.wait()


def body(scalar_field, depth_rank, transfer, light_dir):
    planes, rows, columns = scalar_field.shape
    wide, narrow = lax.axis_size("wide"), lax.axis_size("narrow")
    chips, tiles, part = wide // CORES, rows // SUB, columns // wide
    scale = optical_total / (planes * wide)
    index = lax.axis_index("wide")
    where = jnp.stack([index // CORES, index % CORES]).astype(jnp.int32)
    chunks = CHUNKS if tiles == 8 else (((1, tiles - 2),), ((0, 1), (tiles - 1, 1)))

    smem = pl.BlockSpec(memory_space=pltpu.SMEM)
    vmem = pl.BlockSpec(memory_space=pltpu.VMEM)
    hbm = pl.BlockSpec(memory_space=pltpu.HBM)
    field = pltpu.with_memory_space_constraint(scalar_field, pltpu.HBM)

    def swap(value):
        return lax.ppermute(value, "wide", [(i, i ^ 1) for i in range(wide)])

    def send(value, k):
        return lax.ppermute(value, "wide", [(i, (i + k * CORES) % wide) for i in range(wide)])

    def render(runs, offsets, edges, events, keep=False, given=()):
        slots = sum(min(first + number + 1, tiles) - max(first - 1, 0) for first, number in runs)
        block = pltpu.VMEM((CORES, 4, tiles_of(runs) * SUB, part), jnp.float32)
        buffer = pltpu.VMEM((planes, slots * SUB, columns + 2 * LANE), jnp.float32)
        return call(
            functools.partial(render_kernel, runs, tiles, chips, offsets, scale, len(given)),
            [where, transfer, light_dir, field, *edges, *given],
            [smem] * 3 + [hbm] + [vmem] * (len(edges) + len(given)),
            events,
            out_shape=[block] * len(offsets) + [buffer] * keep,
            out_specs=[vmem] * (len(offsets) + keep),
            scratch_shapes=[buffer] * (not keep and not given) + [pltpu.SemaphoreType.DMA((slots,))],
            cost_estimate=lasting(0.6 * len(offsets) * tiles_of(runs)),
            name="render",
        )

    def edge_rows(events):
        edge = pltpu.VMEM((planes, 1, columns), jnp.float32)
        first_row, last_row = call(
            edges_kernel,
            [field],
            [hbm],
            events,
            out_shape=[edge] * 2,
            out_specs=[vmem] * 2,
            scratch_shapes=[pltpu.SemaphoreType.DMA((2,))],
            cost_estimate=lasting(1.2),
            name="edges",
        )
        up = [(i, i + 1) for i in range(narrow - 1)]
        return lax.ppermute(last_row, "narrow", up), lax.ppermute(first_row, "narrow", [(j, i) for i, j in up])

    def split(arrays, events):
        return call(
            split_kernel,
            arrays,
            [vmem] * len(arrays),
            events,
            out_shape=[pltpu.VMEM((1, *arrays[0].shape[1:]), jnp.float32)] * len(arrays),
            out_specs=[vmem] * len(arrays),
            cost_estimate=lasting(0.3),
            name="split",
        )

    def other_halves(arrays, events, first):
        halves = split(arrays[:first], events)
        if arrays[first:]:
            halves += split(arrays[first:], halves[:1])
        return [swap(value) for value in halves]

    def composite(own, other, runs):
        return call(
            functools.partial(composite_kernel, chips),
            [where, depth_rank, *own, *other],
            [smem] * 2 + [vmem] * (2 * chips),
            out_shape=pltpu.VMEM((3, tiles_of(runs) * SUB, part), jnp.float32),
            out_specs=vmem,
            cost_estimate=lasting(1.0),
            name="composite",
        )

    def across(value, m):
        return lax.ppermute(value, "wide", [(i, i ^ (m * CORES)) for i in range(wide)])

    def gather_by_halves(tile):
        tiles_by, bit = {0: tile}, chips // 2
        while bit:
            tiles_by[bit] = across(tile, bit)
            bit //= 2
        return tiles_by

    def gather_rest(tiles_by, events):
        bits = sorted(tiles_by)[1:]
        held = call(
            relay_kernel,
            [tiles_by[bit] for bit in bits],
            [vmem] * len(bits),
            events,
            out_shape=[pltpu.VMEM(tiles_by[0].shape, jnp.float32)] * len(bits),
            out_specs=[vmem] * len(bits),
            input_output_aliases={i: i for i in range(len(bits))},
            cost_estimate=lasting(0.1),
            name="relay",
        )
        tiles_by = {0: tiles_by[0], **dict(zip(bits, held))}
        for m in range(1, chips):
            low = m & -m
            if m not in tiles_by:
                tiles_by[m] = across(tiles_by[m - low], low)
        order = sorted(tiles_by)
        return [tiles_by[m] for m in order], lambda chip: [jnp.bitwise_xor(chip, m) for m in order]

    def gather_directly(tile):
        values = [tile] + [send(tile, k) for k in range(1, chips)]
        return values, lambda chip: [lax.rem(chip + chips - k, chips) for k in range(chips)]

    early = [tuple(range(chips // 2, 0, -1)), (*range(chips // 2 + 1, chips), 0)]
    sent, near, last, edges = [], [], [], ()
    for i, runs in enumerate(chunks):
        if i == len(chunks) - 1:
            edges = edge_rows(last)
        blocks = {}
        given = ()
        for step, offsets in enumerate(early if i == 0 else [tuple(range(chips))]):
            keep = i == 0 and step == 0
            values = render(runs, offsets, edges, last, keep, given)
            given = values[len(offsets) :] if keep else given
            blocks.update(zip(offsets, values))
            last = list(values[:1])
        near += other_halves([blocks[0]], [], 1)
        sent.append([blocks[0]] + [send(blocks[k], k) for k in range(1, chips)])

    def finish(i, events):
        count = chips // 2 if i == 0 else chips - 1
        other = [near[i]] + other_halves(sent[i][1:], events, count)
        return composite(sent[i], other, chunks[i])

    partial = gather_by_halves(finish(0, last))
    tile = finish(1, [partial[1]])
    groups, finished = [], []
    for runs, (values, chip_of) in zip(chunks, (gather_rest(partial, [tile]), gather_directly(tile))):
        groups.append((runs, chip_of))
        for value in values:
            finished += [value, swap(value)]

    return call(
        functools.partial(place_kernel, groups),
        [where, *finished],
        [smem] + [vmem] * len(finished),
        out_shape=jax.ShapeDtypeStruct((3, rows, columns), jnp.float32),
        out_specs=hbm,
        scratch_shapes=[pltpu.SemaphoreType.DMA((wide * sum(len(runs) for runs, _ in groups),))],
        cost_estimate=lasting(2.0),
        name="place",
    )


def solution(mesh):
    return jax.shard_map(
        body,
        mesh=mesh,
        in_specs=(P("wide", "narrow", None), P(), P(), P()),
        out_specs=P(None, "narrow", None),
        check_vma=False,
    )
```

```python
import functools

import jax
import jax.numpy as jnp
from jax import lax
from jax.experimental import pallas as pl
from jax.experimental.pallas import tpu as pltpu
from jax.sharding import PartitionSpec as P

background = 0.25
optical_total = 2.0

SUB = 8
LANE = 128
CORES = 2
CHUNKS = (((1, 5),), ((0, 1), (6, 1), (7, 1)))
LOG2E = 1.4426950408889634
VMEM_LIMIT = 24 * 2**20


def call(kernel, operands, specs, events=(), **options):
    def with_events(*refs):
        kernel(*refs[: len(operands)], *refs[len(operands) + len(events) :])

    return pl.pallas_call(
        with_events,
        in_specs=list(specs) + [pl.BlockSpec(memory_space=pl.ANY)] * len(events),
        compiler_params=pltpu.CompilerParams(vmem_limit_bytes=VMEM_LIMIT),
        **options,
    )(*operands, *events)


def lasting(microseconds):
    return pl.CostEstimate(flops=0, bytes_accessed=int(microseconds * 3.69e6), transcendentals=0)


def tiles_of(runs):
    return sum(number for _, number in runs)


def edges_kernel(field_ref, first_ref, last_ref, sem):
    rows = field_ref.shape[1]
    copies = [
        pltpu.make_async_copy(field_ref.at[:, pl.ds(row, 1), :], ref, sem.at[i])
        for i, (row, ref) in enumerate(((0, first_ref), (rows - 1, last_ref)))
    ]
    for copy in copies:
        copy.start()
    for copy in copies:
        copy.wait()


def render_kernel(runs, tiles, chips, offsets, scale, given, where_ref, transfer_hbm_ref, light_hbm_ref, field_ref, *refs):
    refs, (transfer_ref, light_ref, small_sem) = refs[:-3], refs[-3:]
    small = [
        pltpu.make_async_copy(source, target, small_sem.at[i])
        for i, (source, target) in enumerate(((transfer_hbm_ref, transfer_ref), (light_hbm_ref, light_ref)))
    ]
    for copy in small:
        copy.start()
    if given:
        edges, padded, out_refs, sem = [], refs[0], refs[1:-1], refs[-1]
    else:
        out_refs, (padded, sem) = refs[-2 - len(offsets) : -2], refs[-2:]
        edges = list(refs[: -2 - len(offsets)])
    planes, _, columns = field_ref.shape
    part = out_refs[0].shape[3]
    my_chip, my_core = where_ref[0], where_ref[1]

    def tile_copy(tile, slot):
        return pltpu.make_async_copy(
            field_ref.at[:, pl.ds(pl.multiple_of(tile * SUB, SUB), SUB), :],
            padded.at[:, pl.ds(pl.multiple_of(slot * SUB, SUB), SUB), pl.ds(LANE, columns)],
            sem.at[slot],
        )

    layout, slot, written = [], 0, 0
    for first, number in runs:
        low, high = max(first - 1, 0), min(first + number + 1, tiles)
        before = edges.pop(0) if first == 0 else None
        behind = edges.pop(0) if first + number == tiles else None
        layout.append((first, number, low, high, slot, written, before, behind))
        for tile in range(low, high) if not given else ():
            tile_copy(tile, slot + tile - low).start()
        slot, written = slot + high - low, written + number
    if not given:
        rim = jnp.zeros((planes, padded.shape[1], LANE), jnp.float32)
        padded[:, :, :LANE] = rim
        padded[:, :, LANE + columns :] = rim

    for copy in small:
        copy.wait()
    light = [0.5 * light_ref[i] for i in range(3)]
    slope = [0.5 * transfer_ref[0, c] for c in range(3)]
    offset = [0.5 * transfer_ref[1, c] for c in range(3)]
    sub = lax.broadcasted_iota(jnp.int32, (SUB, LANE), 0)
    lane = lax.broadcasted_iota(jnp.int32, (SUB, LANE), 1)
    top, bottom = sub == 0, sub == SUB - 1
    leftmost, rightmost = lane == 0, lane == LANE - 1
    vregs = CORES * part // LANE

    def march(slot, out_row, before_ref, behind_ref, column, out_ref):
        def load(plane, shift, vreg):
            ref = {-1: before_ref, 1: behind_ref}.get(shift)
            if ref is not None:
                lanes = pl.ds(pl.multiple_of(column + vreg * LANE, LANE), LANE)
                return jnp.broadcast_to(ref[plane, :, lanes], (SUB, LANE))
            return padded[
                plane,
                pl.ds(pl.multiple_of((slot + shift) * SUB, SUB), SUB),
                pl.ds(pl.multiple_of(column + (1 + vreg) * LANE, LANE), LANE),
            ]

        zero = jnp.zeros((SUB, LANE), jnp.float32)
        depth = [zero] * vregs
        left_over = [zero + 1.0] * vregs
        total = [zero] * vregs
        sums = [[zero] * vregs for _ in range(3)]
        here = [load(0, 0, v) for v in range(-1, vregs + 1)]
        before = here
        for plane in range(planes):
            after = [load(plane + 1, 0, v) for v in range(-1, vregs + 1)] if plane + 1 < planes else here
            for v in range(vregs):
                value = here[v + 1]
                up = pltpu.roll(jnp.where(bottom, load(plane, -1, v), value), 1, 0)
                down = pltpu.roll(jnp.where(top, load(plane, 1, v), value), SUB - 1, 0)
                left = pltpu.roll(jnp.where(rightmost, here[v], value), 1, 1)
                right = pltpu.roll(jnp.where(leftmost, here[v + 2], value), LANE - 1, 1)
                shade = jnp.tanh(
                    light[0] * (after[v + 1] - before[v + 1]) + light[1] * (down - up) + light[2] * (right - left)
                )
                depth[v] = depth[v] + jnp.log2(1.0 + jnp.exp2(value * (2.0 * LOG2E)))
                through = jnp.exp2(depth[v] * -scale)
                lost = left_over[v] - through
                left_over[v] = through
                weight = lost + lost * shade
                total[v] = total[v] + weight
                for c in range(3):
                    sums[c][v] = sums[c][v] + weight * jnp.tanh(slope[c] * value + offset[c])
            before, here = here, after
        for v in range(vregs):
            relative = lax.rem(my_core + v * LANE // part, CORES)
            lanes = pl.ds(v * LANE % part, LANE)
            for c in range(3):
                out_ref[relative, c, pl.ds(out_row, SUB), lanes] = 0.25 * (total[v] + sums[c][v])
            out_ref[relative, 3, pl.ds(out_row, SUB), lanes] = depth[v] * scale

    for step, (k, out_ref) in enumerate(zip(offsets, out_refs)):
        chip = lax.rem(my_chip + k, chips)
        for first, number, low, high, slot, written, before, behind in layout:
            if step == 0 and not given:
                for tile in range(low, min(first + 1, high)):
                    tile_copy(tile, slot + tile - low).wait()

            def one_tile(index, carry, step=step, out_ref=out_ref, chip=chip, run=(first, low, high, slot, written, before, behind)):
                first, low, high, slot, written, before, behind = run
                here = slot + first - low + index

                if step == 0 and not given:

                    @pl.when(first + index + 1 < high)
                    def _():
                        tile_copy(first + index + 1, here + 1).wait()

                out_row = pl.multiple_of((written + index) * SUB, SUB)
                march(here, out_row, before, behind, pl.multiple_of(chip * CORES * part, LANE), out_ref)
                return carry

            lax.fori_loop(0, number, one_tile, 0)


def relay_kernel(*refs):
    del refs


def split_kernel(*refs):
    count = len(refs) // 2
    for block_ref, out_ref in zip(refs[:count], refs[count:]):
        out_ref[...] = block_ref[1:]


def composite_kernel(chips, where_ref, rank_ref, *refs):
    own, other, out_ref = refs[:chips], refs[chips:-1], refs[-1]
    my_chip, my_core = where_ref[0], where_ref[1]
    blocks, ranks = [], []
    for k in range(chips):
        chip = lax.rem(my_chip + chips - k, chips)
        for core, ref in ((my_core, own[k]), (CORES - 1 - my_core, other[k])):
            blocks.append(ref)
            ranks.append(rank_ref[chip * CORES + core])
    bricks = len(ranks)
    ahead = [[(ranks[j] < ranks[i]).astype(jnp.float32) for j in range(bricks)] for i in range(bricks)]
    columns = out_ref.shape[2] // LANE

    def one(index, carry):
        tile = index // columns
        lanes = pl.ds(pl.multiple_of((index - tile * columns) * LANE, LANE), LANE)
        at = (pl.ds(pl.multiple_of(tile * SUB, SUB), SUB), lanes)
        depths = [ref[(0, 3, *at)] for ref in blocks]
        sums = [background * jnp.exp2(-functools.reduce(jnp.add, depths))] * 3
        for i in range(bricks):
            front = functools.reduce(jnp.add, [ahead[i][j] * depths[j] for j in range(bricks) if j != i])
            weight = jnp.exp2(-front)
            for c in range(3):
                sums[c] = sums[c] + weight * blocks[i][(0, c, *at)]
        for c in range(3):
            out_ref[(c, *at)] = sums[c]
        return carry

    lax.fori_loop(0, out_ref.shape[1] // SUB * columns, one, 0)


def place_kernel(groups, where_ref, *refs):
    blocks, out_ref, sem = list(refs[:-2]), refs[-2], refs[-1]
    my_chip, my_core = where_ref[0], where_ref[1]
    copies = []
    for runs, chip_of in groups:
        for chip in chip_of(my_chip):
            for core in (my_core, CORES - 1 - my_core):
                block = blocks.pop(0)
                part = block.shape[2]
                column = pl.multiple_of((chip * CORES + core) * part, LANE)
                written = 0
                for first, number in runs:
                    copy = pltpu.make_async_copy(
                        block.at[:, pl.ds(written * SUB, number * SUB), :],
                        out_ref.at[:, pl.ds(first * SUB, number * SUB), pl.ds(column, part)],
                        sem.at[len(copies)],
                    )
                    copy.start()
                    copies.append(copy)
                    written += number
    for copy in copies:
        copy.wait()


def body(scalar_field, depth_rank, transfer, light_dir):
    planes, rows, columns = scalar_field.shape
    wide, narrow = lax.axis_size("wide"), lax.axis_size("narrow")
    chips, tiles, part = wide // CORES, rows // SUB, columns // wide
    scale = optical_total / (planes * wide)
    index = lax.axis_index("wide")
    where = jnp.stack([index // CORES, index % CORES]).astype(jnp.int32)
    chunks = CHUNKS if tiles == 8 else (((1, tiles - 2),), ((0, 1), (tiles - 1, 1)))

    smem = pl.BlockSpec(memory_space=pltpu.SMEM)
    vmem = pl.BlockSpec(memory_space=pltpu.VMEM)
    hbm = pl.BlockSpec(memory_space=pltpu.HBM)
    field, small_transfer, small_light = [
        pltpu.with_memory_space_constraint(value, pltpu.HBM) for value in (scalar_field, transfer, light_dir)
    ]

    def swap(value):
        return lax.ppermute(value, "wide", [(i, i ^ 1) for i in range(wide)])

    def send(value, k):
        return lax.ppermute(value, "wide", [(i, (i + k * CORES) % wide) for i in range(wide)])

    def render(runs, offsets, edges, events, keep=False, given=()):
        slots = sum(min(first + number + 1, tiles) - max(first - 1, 0) for first, number in runs)
        block = pltpu.VMEM((CORES, 4, tiles_of(runs) * SUB, part), jnp.float32)
        buffer = pltpu.VMEM((planes, slots * SUB, columns + 2 * LANE), jnp.float32)
        return call(
            functools.partial(render_kernel, runs, tiles, chips, offsets, scale, len(given)),
            [where, small_transfer, small_light, field, *edges, *given],
            [smem] + [hbm] * 3 + [vmem] * (len(edges) + len(given)),
            events,
            out_shape=[block] * len(offsets) + [buffer] * keep,
            out_specs=[vmem] * (len(offsets) + keep),
            scratch_shapes=[buffer] * (not keep and not given)
            + [
                pltpu.SemaphoreType.DMA((slots,)),
                pltpu.SMEM(transfer.shape, jnp.float32),
                pltpu.SMEM(light_dir.shape, jnp.float32),
                pltpu.SemaphoreType.DMA((2,)),
            ],
            cost_estimate=lasting(0.6 * len(offsets) * tiles_of(runs)),
            name="render",
        )

    def edge_rows(events):
        edge = pltpu.VMEM((planes, 1, columns), jnp.float32)
        first_row, last_row = call(
            edges_kernel,
            [field],
            [hbm],
            events,
            out_shape=[edge] * 2,
            out_specs=[vmem] * 2,
            scratch_shapes=[pltpu.SemaphoreType.DMA((2,))],
            cost_estimate=lasting(1.2),
            name="edges",
        )
        up = [(i, i + 1) for i in range(narrow - 1)]
        return lax.ppermute(last_row, "narrow", up), lax.ppermute(first_row, "narrow", [(j, i) for i, j in up])

    def split(arrays, events):
        return call(
            split_kernel,
            arrays,
            [vmem] * len(arrays),
            events,
            out_shape=[pltpu.VMEM((1, *arrays[0].shape[1:]), jnp.float32)] * len(arrays),
            out_specs=[vmem] * len(arrays),
            cost_estimate=lasting(0.3),
            name="split",
        )

    def other_halves(arrays, events, first):
        halves = split(arrays[:first], events)
        if arrays[first:]:
            halves += split(arrays[first:], halves[:1])
        return [swap(value) for value in halves]

    def composite(own, other, runs):
        return call(
            functools.partial(composite_kernel, chips),
            [where, depth_rank, *own, *other],
            [smem] * 2 + [vmem] * (2 * chips),
            out_shape=pltpu.VMEM((3, tiles_of(runs) * SUB, part), jnp.float32),
            out_specs=vmem,
            cost_estimate=lasting(1.0),
            name="composite",
        )

    def across(value, m):
        return lax.ppermute(value, "wide", [(i, i ^ (m * CORES)) for i in range(wide)])

    def gather_by_halves(tile):
        tiles_by, bit = {0: tile}, chips // 2
        while bit:
            tiles_by[bit] = across(tile, bit)
            bit //= 2
        return tiles_by

    def gather_rest(tiles_by, events):
        bits = sorted(tiles_by)[1:]
        held = call(
            relay_kernel,
            [tiles_by[bit] for bit in bits],
            [vmem] * len(bits),
            events,
            out_shape=[pltpu.VMEM(tiles_by[0].shape, jnp.float32)] * len(bits),
            out_specs=[vmem] * len(bits),
            input_output_aliases={i: i for i in range(len(bits))},
            cost_estimate=lasting(0.1),
            name="relay",
        )
        tiles_by = {0: tiles_by[0], **dict(zip(bits, held))}
        for m in range(1, chips):
            low = m & -m
            if m not in tiles_by:
                tiles_by[m] = across(tiles_by[m - low], low)
        order = sorted(tiles_by)
        return [tiles_by[m] for m in order], lambda chip: [jnp.bitwise_xor(chip, m) for m in order]

    def gather_directly(tile):
        values = [tile] + [send(tile, k) for k in range(1, chips)]
        return values, lambda chip: [lax.rem(chip + chips - k, chips) for k in range(chips)]

    early = [tuple(range(chips // 2, 0, -1)), (*range(chips // 2 + 1, chips), 0)]
    sent, near, last, edges = [], [], [], ()
    for i, runs in enumerate(chunks):
        if i == len(chunks) - 1:
            edges = edge_rows(last)
        blocks = {}
        given = ()
        for step, offsets in enumerate(early if i == 0 else [tuple(range(chips))]):
            keep = i == 0 and step == 0
            values = render(runs, offsets, edges, last, keep, given)
            given = values[len(offsets) :] if keep else given
            blocks.update(zip(offsets, values))
            last = list(values[:1])
        near += other_halves([blocks[0]], [], 1)
        sent.append([blocks[0]] + [send(blocks[k], k) for k in range(1, chips)])

    def finish(i, events):
        count = chips // 2 if i == 0 else chips - 1
        other = [near[i]] + other_halves(sent[i][1:], events, count)
        return composite(sent[i], other, chunks[i])

    partial = gather_by_halves(finish(0, last))
    tile = finish(1, [partial[1]])
    groups, finished = [], []
    for runs, (values, chip_of) in zip(chunks, (gather_rest(partial, [tile]), gather_directly(tile))):
        groups.append((runs, chip_of))
        for value in values:
            finished += [value, swap(value)]

    return call(
        functools.partial(place_kernel, groups),
        [where, *finished],
        [smem] + [vmem] * len(finished),
        out_shape=jax.ShapeDtypeStruct((3, rows, columns), jnp.float32),
        out_specs=hbm,
        scratch_shapes=[pltpu.SemaphoreType.DMA((wide * sum(len(runs) for runs, _ in groups),))],
        cost_estimate=lasting(2.0),
        name="place",
    )


def solution(mesh):
    return jax.shard_map(
        body,
        mesh=mesh,
        in_specs=(P("wide", "narrow", None), P(), P(), P()),
        out_specs=P(None, "narrow", None),
        check_vma=False,
    )
```
